128 devices in a mesh: leaf: 32 (over y, z, core), sub: 4 (over x).
Axes of the slice: x: 4, y: 4, z: 4, core: 2. Of those that a mesh axis runs over, the one named last changes fastest.
Arguments:
- multipoles: bfloat16 [456, 65536], P(None, ('leaf', 'sub')), may hold values from -6 to 6
- m2l_ops: bfloat16 [456, 44, 456], replicated, may hold values from -0.0390625 to 0.0390625
- m2m_ops: bfloat16 [456, 8, 456], replicated, may hold values from -0.09375 to 0.09375
- l2l_ops: bfloat16 [8, 456, 456], replicated, may hold values from -0.25 to 0.25
- ghost_rows: int32 [128, 26, 64], P(('leaf', 'sub')), may hold values from 0 to 511
- source_slot: int32 [128, 44, 512], P(('leaf', 'sub')), may hold values from 0 to 2175
- pair_mask: int32 [128, 44, 512], P(('leaf', 'sub')), may hold values 0 or 1
- coarse_src: int32 [1024, 44], P(('leaf', 'sub')), may hold values from 0 to 1023
- coarse_mask: int32 [1024, 44], P(('leaf', 'sub')), may hold values 0 or 1
Outputs:
- locals_fine: bfloat16 [456, 65536], P(None, ('leaf', 'sub'))
The draws below stay inside these ranges and needn't reach their ends.
All inputs are finite; a program needn't handle non-finite values. No bound on the sum of `pair_mask` or of `coarse_mask` on one device may be relied on, other than what follows from the above.
Results may differ from the reference program's by a relative error of at most 0.006.
Values may be sent and summed in bfloat16 or wider, within the bound.
A program may use at most 192 MiB of HBM per device.

```python
import jax
import jax.numpy as jnp
from jax import lax

COEF = 456
OPS = 44
NEIGH = 26
BOX_DEV = 512
GHOST = 64
RANKS = 128
NA = 65536
NC = 1024
SLOTS = 2176


def plant(values, own_key, smallest, high):
    shape = values.shape
    spot = [jax.random.randint(jax.random.fold_in(own_key, axis), (), 0, shape[axis]) for axis in range(len(shape))]
    values = values.at[tuple(spot)].set(smallest)
    longest = shape.index(max(shape))
    spot[longest] = (spot[longest] + 1) % shape[longest]
    return values.at[tuple(spot)].set(high)


def block_scale(rng, shape, shards, smallest, largest):
    def one(position, shards_of):
        steps = jax.random.uniform(jax.random.fold_in(jax.random.fold_in(rng, 6), position), (shards_of,), jnp.float32, smallest / len(shards), largest / len(shards))
        return jnp.repeat(jnp.exp(steps), shape[position] // shards_of).reshape((-1,) + (1,) * (len(shape) - position - 1))

    loudness = one(*shards[0])
    for cut in shards[1:]:
        loudness = loudness * one(*cut)
    return loudness


def scatter_about(key, dims, width, most, pieces=(), kind=jnp.bfloat16):
    drawn = width * jax.random.normal(key, dims, jnp.float32)
    if pieces:
        drawn = drawn * block_scale(key, dims, pieces, -0.22, 0.18)
    return jnp.clip(drawn, -most, most).astype(kind)


def setup_inputs(seed: int = 0) -> dict:
    arg_keys = jax.random.split(jax.random.key(seed), 10)
    multipoles = scatter_about(arg_keys[0], (COEF, NA), 1.0, 6.0, ((1, 128),))
    m2l_ops = scatter_about(arg_keys[1], (COEF, OPS, COEF), (OPS * COEF) ** -0.5, 0.0390625)
    m2m_ops = scatter_about(arg_keys[2], (COEF, 8, COEF), (8 * COEF) ** -0.5, 0.09375)
    l2l_ops = scatter_about(arg_keys[3], (8, COEF, COEF), COEF ** -0.5, 0.25)
    ghost_rows = plant(jax.random.randint(arg_keys[4], (RANKS, NEIGH, GHOST), 0, BOX_DEV), jax.random.fold_in(arg_keys[4], 1), 0, BOX_DEV - 1).astype(jnp.int32)
    source_slot = plant(jax.random.randint(arg_keys[5], (RANKS, OPS, BOX_DEV), 0, SLOTS), jax.random.fold_in(arg_keys[5], 1), 0, SLOTS - 1).astype(jnp.int32)
    pair_mask = plant((jax.random.randint(arg_keys[6], (RANKS, OPS, BOX_DEV), 0, 4) < 3).astype(jnp.int32), jax.random.fold_in(arg_keys[6], 1), 0, 1)
    coarse_src = plant(jax.random.randint(arg_keys[7], (NC, OPS), 0, NC), jax.random.fold_in(arg_keys[7], 1), 0, NC - 1).astype(jnp.int32)
    coarse_mask = plant((jax.random.randint(arg_keys[8], (NC, OPS), 0, 4) < 3).astype(jnp.int32), jax.random.fold_in(arg_keys[8], 1), 0, 1)
    return dict(multipoles=multipoles, m2l_ops=m2l_ops, m2m_ops=m2m_ops, l2l_ops=l2l_ops, ghost_rows=ghost_rows, source_slot=source_slot, pair_mask=pair_mask, coarse_src=coarse_src, coarse_mask=coarse_mask)


def directions():
    found = []
    for step_a in (-1, 0, 1):
        for step_b in (-1, 0, 1):
            for step_c in (-1, 0, 1):
                if step_a != 0 or step_b != 0 or step_c != 0:
                    found.append(16 * step_a + 4 * step_b + step_c)
    return found


def upward(child, m2m_ops):
    grouped = child.astype(jnp.float32).reshape(COEF, child.shape[1] // 8, 8)
    return jnp.einsum('oki,ipk->op', m2m_ops.astype(jnp.float32), grouped).astype(jnp.bfloat16)


def downward(parent, l2l_ops):
    spread = jnp.einsum('koi,ip->opk', l2l_ops.astype(jnp.float32), parent.astype(jnp.float32))
    return spread.reshape(COEF, parent.shape[1] * 8)


def translate(columns, m2l_ops, present):
    weighted = columns.astype(jnp.float32) * present.astype(jnp.float32)[None]
    return jnp.einsum('aoi,ion->an', m2l_ops.astype(jnp.float32), weighted)


def reference(multipoles, m2l_ops, m2m_ops, l2l_ops, ghost_rows, source_slot, pair_mask, coarse_src, coarse_mask):
    m_mid = upward(multipoles, m2m_ops)
    m_top = upward(m_mid, m2m_ops)
    coarse_cols = m_top[:, coarse_src.T]
    l_top = (0.25 * translate(coarse_cols, m2l_ops, coarse_mask.T)).astype(jnp.bfloat16)
    l_mid = downward(l_top, l2l_ops).astype(jnp.bfloat16)
    steps = jnp.array(directions(), dtype=jnp.int32)
    which = jnp.arange(NEIGH, dtype=jnp.int32)

    def one_device(device):
        start = (device * BOX_DEV).astype(jnp.int32)
        own = lax.dynamic_slice_in_dim(multipoles, start, BOX_DEV, 1)
        owners = jnp.mod(device + steps, RANKS).astype(jnp.int32)
        rows = ghost_rows[owners, which]
        flat = (rows + (owners * BOX_DEV)[:, None]).reshape(-1)
        combined = jnp.concatenate([own, multipoles[:, flat]], axis=1)
        near = translate(combined[:, source_slot[device]], m2l_ops, pair_mask[device])
        parent = lax.dynamic_slice_in_dim(l_mid, (device * (BOX_DEV // 8)).astype(jnp.int32), BOX_DEV // 8, 1)
        return (near + downward(parent, l2l_ops)).astype(jnp.bfloat16)

    blocks = lax.map(one_device, jnp.arange(RANKS, dtype=jnp.int32))
    return jnp.transpose(blocks, (1, 0, 2)).reshape(COEF, NA)
```

```python
import functools

import jax
import jax.numpy as jnp
from jax import lax
from jax.experimental import pallas as pl
from jax.experimental.pallas import tpu as pltpu
from jax.sharding import PartitionSpec as P

MESH = pl.DeviceIdType.MESH
COEF = 456
WIDE = 512
ROWS = 464
OPS = 44
BOXES = 512
GHOST = 64
DIRS = 26
RANKS = 128
SLOTS = 2176
EMPTY = SLOTS
TOP = SLOTS + 8
TOPS = 1024
TABLE = TOP + TOPS
TARGETS = BOXES + 8
PADDED = 528
BLOCK = 48
BLOCKS = 10
LAST = BLOCKS - 1
TAIL = COEF - LAST * BLOCK
F32 = jnp.float32
BF16 = jnp.bfloat16


def place(d):
    return (d // 4, d % 4)


def chunk_width(j):
    return min(128, COEF - 128 * j)


def regroup(load, store, scratch, classes):
    for first in range(0, classes, 8):
        here = min(8, classes - first)
        for j in range(4):
            wide = chunk_width(j)
            part = load(first, here, j, wide).astype(F32)
            if here < 8:
                part = jnp.concatenate([part, jnp.zeros((BLOCK, 8 - here, wide), F32)], axis=1)
            scratch[j][:, 0:wide] = part.reshape(BLOCK * 8, wide)
        for o in range(here):
            for j in range(4):
                store(first + o, j, scratch[j][pl.ds(o, BLOCK, stride=8), :].astype(BF16))


def nt(left, right):
    return lax.dot_general(left, right, (((1,), (1,)), ((), ())), preferred_element_type=F32)


def prep(
    x,
    gh,
    m2m,
    m2l,
    wt,
    own_out,
    ghost,
    mt,
    own,
    send,
    m2m_vm,
    wm,
    stage,
    wst,
    r0,
    r1,
    r2,
    r3,
    mid0,
    mid1,
    mid2,
    mid3,
    top,
    topb,
    g_send,
    g_recv,
    a_send,
    a_recv,
    in_sem,
    out_sem,
    misc,
):
    leaf = lax.axis_index("leaf")
    sx = lax.axis_index("sub")
    me = leaf * 4 + sx
    core = leaf % 2
    yz = leaf // 2
    sz = yz % 4
    sy = yz // 4
    regroup_scratch = (r0, r1, r2, r3)
    mids = (mid0, mid1, mid2, mid3)

    def direction(i):
        return i - 9 if i >= 18 else (i // 2 if i % 2 == 0 else 17 + i // 2)

    def offset(j):
        k = j + jnp.where(j >= 13, 1, 0)
        return 16 * (k // 9 - 1) + 4 * ((k // 3) % 3 - 1) + (k % 3 - 1)

    def reader(j):
        return place((me - offset(j) + RANKS) % RANKS)

    def group_peer(stage_number, step):
        if stage_number == 0:
            return (leaf, (sx + step) % 4)
        if stage_number == 1:
            return ((sy * 4 + (sz + step) % 4) * 2 + core, sx)
        if stage_number == 2:
            return ((((sy + step) % 4) * 4 + sz) * 2 + core, sx)
        return (yz * 2 + (1 - core), sx)

    steps = [(0, 1), (0, 2), (0, 3), (1, 1), (1, 2), (1, 3), (2, 1), (2, 2), (2, 3), (3, 1)]

    barrier = pltpu.get_barrier_semaphore()

    def greet(i, carry):
        pl.semaphore_signal(barrier, inc=1, device_id=reader(i), device_id_type=MESH)
        return carry

    lax.fori_loop(0, DIRS, greet, 0)
    for number, step in steps:
        pl.semaphore_signal(barrier, inc=1, device_id=group_peer(number, step), device_id_type=MESH)

    def block_in(b, slot, rows):
        return pltpu.make_async_copy(
            m2l.at[pl.ds(b * BLOCK, rows)], stage.at[slot, pl.ds(0, rows)], in_sem.at[slot]
        )

    def block_out(b, slot, rows):
        return pltpu.make_async_copy(
            wst.at[slot, :, pl.ds(0, rows)], wt.at[:, pl.ds(b * BLOCK, rows)], out_sem.at[slot]
        )

    m2m_copy = pltpu.make_async_copy(m2m, m2m_vm.at[pl.ds(0, COEF)], misc.at[0])
    m2m_copy.start()
    block_in(0, 0, BLOCK).start()
    block_in(1, 1, BLOCK).start()

    whole = jnp.concatenate([x[...].astype(F32), jnp.zeros((WIDE - COEF, BOXES), F32)], axis=0).T
    for j in range(4):
        own[pl.ds(j, BOXES, stride=4), :] = whole[:, 128 * j : 128 * (j + 1)]
    own_copy = pltpu.make_async_copy(own, own_out, misc.at[1])
    own_copy.start()
    r3[...] = jnp.zeros_like(r3)
    mid3[...] = jnp.zeros_like(mid3)
    top[...] = jnp.zeros_like(top)
    m2m_vm[COEF : BLOCK * BLOCKS] = jnp.zeros((BLOCK * BLOCKS - COEF, 8, COEF), BF16)

    pl.semaphore_wait(barrier, DIRS + len(steps))

    def ghost_copy(j):
        return pltpu.make_async_remote_copy(
            src_ref=send.at[j],
            dst_ref=ghost.at[pl.ds(j * GHOST, GHOST)],
            send_sem=g_send.at[j],
            recv_sem=g_recv.at[j],
            device_id=reader(j),
            device_id_type=MESH,
        )

    order = [direction(i) for i in range(DIRS)]
    columns = whole.astype(BF16)
    lanes = lax.broadcasted_iota(jnp.int32, (GHOST, BOXES), 1)
    for first in range(0, DIRS, 4):
        group = order[first : first + 4]
        chosen = [(gh[:, j : j + 1] == lanes).astype(F32).astype(BF16) for j in group]
        rows = jnp.dot(jnp.concatenate(chosen, axis=0), columns, preferred_element_type=F32)
        for n, j in enumerate(group):
            send[j] = rows[GHOST * n : GHOST * (n + 1)].astype(BF16)
            ghost_copy(j).start()

    m2m_copy.wait()

    def regroup_m2m(b, carry):
        start = pl.multiple_of(b * BLOCK, BLOCK)
        regroup(
            lambda first, here, j, wide: m2m_vm[
                pl.ds(start, BLOCK), pl.ds(first, here), pl.ds(128 * j, wide)
            ],
            lambda o, j, value: wm.__setitem__(
                (o, pl.ds(start, BLOCK), pl.ds(128 * j, 128)), value
            ),
            regroup_scratch,
            8,
        )
        return carry

    lax.fori_loop(0, BLOCKS, regroup_m2m, 0)

    total = jnp.zeros((64, ROWS), F32)
    for k in range(8):
        rows = [own[pl.ds(4 * k + j, 64, stride=32), :].astype(BF16) for j in range(4)]
        total += nt(jnp.concatenate(rows, axis=1), wm[k, 0:ROWS, :])
    total = total.astype(BF16).astype(F32)
    for j in range(4):
        wide = min(128, ROWS - 128 * j)
        mids[j][:, 0:wide] = total[:, 128 * j : 128 * j + wide]
    total = jnp.zeros((8, ROWS), F32)
    for k in range(8):
        rows = [mids[j][pl.ds(k, 8, stride=8), :].astype(BF16) for j in range(4)]
        total += nt(jnp.concatenate(rows, axis=1), wm[k, 0:ROWS, :])
    for j in range(4):
        wide = min(128, ROWS - 128 * j)
        top[pl.ds(j, 8, stride=4), 0:wide] = total[:, 128 * j : 128 * j + wide]
    topb[...] = top[...].astype(BF16)

    mine = pltpu.make_async_copy(topb, mt.at[yz, core, pl.ds(sx * 32, 32)], misc.at[2])
    mine.start()

    def gather_copy(number, step):
        if number == 0:
            src, dst = topb, mt.at[yz, core, pl.ds(sx * 32, 32)]
        elif number == 1:
            src = dst = mt.at[yz, core]
        elif number == 2:
            src = dst = mt.at[pl.ds(sy * 4, 4), core]
        else:
            src = dst = mt.at[:, core]
        index = number * 3 + step - 1
        return pltpu.make_async_remote_copy(
            src_ref=src,
            dst_ref=dst,
            send_sem=a_send.at[index],
            recv_sem=a_recv.at[index],
            device_id=group_peer(number, step),
            device_id_type=MESH,
        )

    for step in (1, 2, 3):
        gather_copy(0, step).start()

    def next_stage(number):
        for step in (1, 2, 3):
            gather_copy(number - 1, step).wait()
        if number == 1:
            mine.wait()
        for step in (1, 2, 3) if number < 3 else (1,):
            gather_copy(number, step).start()

    def regroup_m2l(b, carry):
        slot = b % 2

        @pl.when(b < LAST)
        def _():
            block_in(b, slot, BLOCK).wait()

        @pl.when(b == LAST)
        def _():
            block_in(b, slot, TAIL).wait()

        @pl.when(b >= 2)
        def _():
            block_out(b - 2, slot, BLOCK).wait()

        regroup(
            lambda first, here, j, wide: stage[
                slot, :, pl.ds(first, here), pl.ds(128 * j, wide)
            ],
            lambda o, j, value: wst.__setitem__((slot, o, slice(None), pl.ds(128 * j, 128)), value),
            regroup_scratch,
            OPS,
        )

        @pl.when(b + 2 < LAST)
        def _():
            block_in(b + 2, slot, BLOCK).start()

        @pl.when(b + 2 == LAST)
        def _():
            block_in(b + 2, slot, TAIL).start()

        @pl.when(b < LAST)
        def _():
            block_out(b, slot, BLOCK).start()

        @pl.when(b == LAST)
        def _():
            block_out(b, slot, ROWS - LAST * BLOCK).start()

        for number, when in ((1, 1), (2, 3), (3, 6)):

            @pl.when(b == when)
            def _():
                next_stage(number)

        return carry

    lax.fori_loop(0, BLOCKS, regroup_m2l, 0)

    gather_copy(3, 1).wait()
    own_copy.wait()
    block_out(LAST - 1, (LAST - 1) % 2, BLOCK).wait()
    block_out(LAST, LAST % 2, ROWS - LAST * BLOCK).wait()

    def settle(j, carry):
        ghost_copy(j).wait()
        return carry

    lax.fori_loop(0, DIRS, settle, 0)


def prepare(multipoles, ghost_rows, m2m_ops, m2l_ops):
    any_space = pl.BlockSpec(memory_space=pl.ANY)
    return pl.pallas_call(
        prep,
        out_shape=(
            jax.ShapeDtypeStruct((OPS, ROWS, WIDE), BF16),
            jax.ShapeDtypeStruct((4 * BOXES, 128), F32),
            jax.ShapeDtypeStruct((GHOST * DIRS, WIDE), BF16),
            jax.ShapeDtypeStruct((16, 2, 128, 128), BF16),
        ),
        in_specs=[
            pl.BlockSpec(memory_space=pltpu.VMEM),
            pl.BlockSpec(memory_space=pltpu.VMEM),
            any_space,
            any_space,
        ],
        out_specs=(any_space,) * 4,
        scratch_shapes=[
            pltpu.VMEM((4 * BOXES, 128), F32),
            pltpu.VMEM((DIRS, GHOST, WIDE), BF16),
            pltpu.VMEM((BLOCK * BLOCKS, 8, COEF), BF16),
            pltpu.VMEM((8, BLOCK * BLOCKS, WIDE), BF16),
            pltpu.VMEM((2, BLOCK, OPS, COEF), BF16),
            pltpu.VMEM((2, OPS, BLOCK, WIDE), BF16),
        ]
        + [pltpu.VMEM((8 * BLOCK, 128), F32)] * 4
        + [pltpu.VMEM((64, 128), F32)] * 4
        + [
            pltpu.VMEM((32, 128), F32),
            pltpu.VMEM((32, 128), BF16),
            pltpu.SemaphoreType.DMA((DIRS,)),
            pltpu.SemaphoreType.DMA((DIRS,)),
            pltpu.SemaphoreType.DMA((10,)),
            pltpu.SemaphoreType.DMA((10,)),
            pltpu.SemaphoreType.DMA((2,)),
            pltpu.SemaphoreType.DMA((2,)),
            pltpu.SemaphoreType.DMA((3,)),
        ],
        compiler_params=pltpu.CompilerParams(
            collective_id=0, has_side_effects=True, vmem_limit_bytes=48 * 2**20
        ),
    )(multipoles, ghost_rows, m2m_ops, m2l_ops)


def translate(idx, own, ghost, mt, wt, l2l, out, table, even, odd, acc, f0, f1, f2, f3):
    s = pl.program_id(0)
    far = (f0, f1, f2, f3)

    def collect(pair, buf):
        for q in range(2):
            o = pair * 2 + q
            for first in range(0, TARGETS, 8):
                rows = [
                    table[pl.ds(pl.multiple_of(idx[o, first + u], 4), 4), :] for u in range(8)
                ]
                for u in range(8):
                    buf[q, pl.ds(4 * (first + u), 4), :] = rows[u]

    def multiply(buf, first):
        left = [
            buf[q, pl.ds(j, PADDED, stride=4), :].astype(BF16) for q in range(2) for j in range(4)
        ]
        right = [wt[first + q] for q in range(2)]
        acc[...] += nt(jnp.concatenate(left, axis=1), jnp.concatenate(right, axis=1))

    @pl.when(s == 0)
    def _():
        even[...] = jnp.zeros_like(even)
        odd[...] = jnp.zeros_like(odd)
        acc[...] = jnp.zeros_like(acc)
        table[0 : 4 * BOXES, :] = own[...]
        for j in range(4):
            received = ghost[:, 128 * j : 128 * (j + 1)].astype(F32)
            table[pl.ds(4 * BOXES + j, GHOST * DIRS, stride=4), :] = received
        table[4 * EMPTY : 4 * TOP, :] = jnp.zeros((4 * (TOP - EMPTY), 128), F32)
        table[4 * TOP : 4 * TABLE, :] = mt[...].astype(F32)
        collect(0, even)

    collect(2 * s + 1, odd)
    multiply(even, 0)

    @pl.when(s < OPS // 4 - 1)
    def _():
        collect(2 * s + 2, even)
        multiply(odd, 2)

    @pl.when(s == OPS // 4 - 1)
    def _():
        multiply(odd, 2)
        l_top = (0.25 * acc[BOXES:PADDED, 0:COEF]).astype(BF16)
        for k in range(8):
            part = nt(l_top, l2l[k])[0:8]
            for j in range(4):
                wide = chunk_width(j)
                far[j][pl.ds(k, 8, stride=8), 0:wide] = part[:, 128 * j : 128 * j + wide]
        l_mid = jnp.concatenate([far[j][0:64, 0 : chunk_width(j)] for j in range(4)], axis=1)
        l_mid = l_mid.astype(BF16)
        for k in range(8):
            part = nt(l_mid, l2l[k])
            for j in range(4):
                wide = chunk_width(j)
                far[j][pl.ds(k, 64, stride=8), 0:wide] = part[:, 128 * j : 128 * j + wide]
        for j in range(4):
            wide = chunk_width(j)
            near = acc[0:BOXES, 128 * j : 128 * j + wide]
            both = near + far[j][:, 0:wide]
            out[128 * j : 128 * j + wide, :] = both.T.astype(BF16)


def apply_near(idx, own, ghost, mt, wt, l2l_ops):
    return pl.pallas_call(
        translate,
        grid=(OPS // 4,),
        out_shape=jax.ShapeDtypeStruct((COEF, BOXES), BF16),
        in_specs=[
            pl.BlockSpec(memory_space=pltpu.SMEM),
            pl.BlockSpec(own.shape, lambda s: (0, 0)),
            pl.BlockSpec(ghost.shape, lambda s: (0, 0)),
            pl.BlockSpec(mt.shape, lambda s: (0, 0)),
            pl.BlockSpec((4, ROWS, WIDE), lambda s: (s, 0, 0)),
            pl.BlockSpec(l2l_ops.shape, lambda s: (0, 0, 0)),
        ],
        out_specs=pl.BlockSpec((COEF, BOXES), lambda s: (0, 0)),
        scratch_shapes=[pltpu.VMEM((4 * TABLE, 128), F32)]
        + [pltpu.VMEM((2, 4 * PADDED, 128), F32)] * 2
        + [pltpu.VMEM((PADDED, ROWS), F32)]
        + [pltpu.VMEM((BOXES, 128), F32)] * 4,
        compiler_params=pltpu.CompilerParams(vmem_limit_bytes=56 * 2**20),
    )(idx, own, ghost, mt, wt, l2l_ops)


def local(
    multipoles,
    m2l_ops,
    m2m_ops,
    l2l_ops,
    ghost_rows,
    source_slot,
    pair_mask,
    coarse_src,
    coarse_mask,
):
    near_idx = jnp.where(pair_mask[0] == 1, source_slot[0], EMPTY)
    top_idx = jnp.where(coarse_mask == 1, coarse_src + TOP, EMPTY).T
    idx = 4 * jnp.concatenate([near_idx, top_idx], axis=1)
    wt, own, ghost, mt = prepare(multipoles, ghost_rows[0].T, m2m_ops, m2l_ops)
    return apply_near(idx, own, ghost, mt.reshape(4 * TOPS, 128), wt, l2l_ops)


def solution(mesh):
    both = ("leaf", "sub")
    return jax.shard_map(
        local,
        mesh=mesh,
        in_specs=(
            P(None, both),
            P(),
            P(),
            P(),
            P(both, None, None),
            P(both, None, None),
            P(both, None, None),
            P(both, None),
            P(both, None),
        ),
        out_specs=P(None, both),
        check_vma=False,
    )
```

```python
import functools

import jax
import jax.numpy as jnp
from jax import lax
from jax.experimental import pallas as pl
from jax.experimental.pallas import tpu as pltpu
from jax.sharding import PartitionSpec as P

MESH = pl.DeviceIdType.MESH
COEF = 456
WIDE = 512
ROWS = 464
OPS = 44
BOXES = 512
GHOST = 64
DIRS = 26
RANKS = 128
SLOTS = 2176
EMPTY = SLOTS
TABLE = SLOTS + 8
TOPS = 1024
BLOCK = 48
BLOCKS = 10
CHUNK = 4
CHUNKS = OPS // CHUNK
ORDER = [j for i in range(9) for j in (i, 17 + i, 9 + i)][:DIRS]
F32 = jnp.float32
BF16 = jnp.bfloat16


def place(d):
    return (d // 4, d % 4)


def chunk_width(j):
    return min(128, COEF - 128 * j)


def regroup(load, store, scratch, classes):
    for first in range(0, classes, 8):
        here = min(8, classes - first)
        for j in range(4):
            wide = chunk_width(j)
            part = load(first, here, j, wide).astype(F32)
            if here < 8:
                part = jnp.concatenate([part, jnp.zeros((BLOCK, 8 - here, wide), F32)], axis=1)
            scratch[j][:, 0:wide] = part.reshape(BLOCK * 8, wide)
        for o in range(here):
            for j in range(4):
                store(first + o, j, scratch[j][pl.ds(o, BLOCK, stride=8), :].astype(BF16))


def widen(w):
    tail = jnp.concatenate([w[:, 384:COEF], jnp.zeros((COEF, WIDE - COEF), BF16)], axis=1)
    return jnp.concatenate([w[:, 0:384], tail], axis=1)


def nt(left, right):
    return lax.dot_general(left, right, (((1,), (1,)), ((), ())), preferred_element_type=F32)


def prep(
    x_hbm,
    gh_hbm,
    slot_hbm,
    mask_hbm,
    csrc_hbm,
    cmask_hbm,
    m2m,
    m2l,
    l2l,
    own_hbm,
    idx_hbm,
    far_hbm,
    ghost,
    x,
    gh,
    slot,
    mask,
    csrc,
    cmask,
    own,
    idx,
    far,
    send,
    m2m_vm,
    wm,
    l2l_vm,
    w,
    picks,
    r0,
    r1,
    r2,
    r3,
    mid0,
    mid1,
    mid2,
    mid3,
    top,
    topb,
    mt,
    wide_top,
    g_send,
    g_recv,
    a_send,
    a_recv,
    in_sem,
    out_sem,
    misc,
):
    leaf = lax.axis_index("leaf")
    sx = lax.axis_index("sub")
    me = leaf * 4 + sx
    core = leaf % 2
    yz = leaf // 2
    sz = yz % 4
    sy = yz // 4
    regroup_scratch = (r0, r1, r2, r3)
    mids = (mid0, mid1, mid2, mid3)

    def offset(j):
        k = j + jnp.where(j >= 13, 1, 0)
        return 16 * (k // 9 - 1) + 4 * ((k // 3) % 3 - 1) + (k % 3 - 1)

    def reader(j):
        return place((me - offset(j) + RANKS) % RANKS)

    def group_peer(stage_number, step):
        if stage_number == 0:
            return ((sy * 4 + (sz + step) % 4) * 2 + core, sx)
        if stage_number == 1:
            return (leaf, (sx + step) % 4)
        if stage_number == 2:
            return ((((sy + step) % 4) * 4 + sz) * 2 + core, sx)
        return (yz * 2 + (1 - core), sx)

    steps = [(0, 1), (0, 2), (0, 3), (1, 1), (1, 2), (1, 3), (2, 1), (2, 2), (2, 3), (3, 1)]

    barrier = pltpu.get_barrier_semaphore()

    def greet(i, carry):
        pl.semaphore_signal(barrier, inc=1, device_id=reader(i), device_id_type=MESH)
        return carry

    lax.fori_loop(0, DIRS, greet, 0)
    for number, step in steps:
        pl.semaphore_signal(barrier, inc=1, device_id=group_peer(number, step), device_id_type=MESH)

    given = (x_hbm, gh_hbm, slot_hbm, mask_hbm, csrc_hbm, cmask_hbm)
    small = [
        pltpu.make_async_copy(source, target, in_sem.at[n])
        for n, (source, target) in enumerate(zip(given, (x, gh, slot, mask, csrc, cmask)))
    ]
    for copy in small:
        copy.start()
    m2m_copy = pltpu.make_async_copy(m2m, m2m_vm.at[pl.ds(0, COEF)], misc.at[0])
    m2m_copy.start()
    w_copy = pltpu.make_async_copy(m2l, w, misc.at[3])
    w_copy.start()
    l2l_copy = pltpu.make_async_copy(l2l, l2l_vm, misc.at[1])
    l2l_copy.start()

    r3[...] = jnp.zeros_like(r3)
    mid3[...] = jnp.zeros_like(mid3)
    top[...] = jnp.zeros_like(top)
    m2m_vm[COEF : BLOCK * BLOCKS] = jnp.zeros((BLOCK * BLOCKS - COEF, 8, COEF), BF16)

    picks[...] = jnp.zeros_like(picks)
    for copy in small:
        copy.wait()
    for j in range(DIRS):
        picks[j : j + 1, 0:GHOST] = gh[j].astype(F32)
    by_direction = picks[...].T[0:GHOST]
    whole = jnp.concatenate([x[...].astype(F32), jnp.zeros((WIDE - COEF, BOXES), F32)], axis=0).T
    for j in range(4):
        own[pl.ds(j, BOXES, stride=4), :] = whole[:, 128 * j : 128 * (j + 1)]
    idx[...] = 4 * jnp.where(mask[...] == 1, slot[...], EMPTY)
    own_copy = pltpu.make_async_copy(own, own_hbm, out_sem.at[0])
    idx_copy = pltpu.make_async_copy(idx, idx_hbm, out_sem.at[1])
    own_copy.start()
    idx_copy.start()

    pl.semaphore_wait(barrier, DIRS + len(steps))

    def ghost_copy(j):
        return pltpu.make_async_remote_copy(
            src_ref=send.at[j],
            dst_ref=ghost.at[pl.ds(j * GHOST, GHOST)],
            send_sem=g_send.at[j],
            recv_sem=g_recv.at[j],
            device_id=reader(j),
            device_id_type=MESH,
        )

    columns = whole.astype(BF16)
    lanes = lax.broadcasted_iota(jnp.int32, (GHOST, BOXES), 1).astype(F32)

    def give(first, last):
        group = ORDER[first:last]
        chosen = [(by_direction[:, j : j + 1] == lanes).astype(F32).astype(BF16) for j in group]
        rows = jnp.dot(jnp.concatenate(chosen, axis=0), columns, preferred_element_type=F32)
        for n, j in enumerate(group):
            send[j] = rows[GHOST * n : GHOST * (n + 1)].astype(BF16)
            ghost_copy(j).start()

    give(0, 6)
    m2m_copy.wait()

    def regroup_m2m(b, carry):
        start = pl.multiple_of(b * BLOCK, BLOCK)
        regroup(
            lambda first, here, j, wide: m2m_vm[
                pl.ds(start, BLOCK), pl.ds(first, here), pl.ds(128 * j, wide)
            ],
            lambda o, j, value: wm.__setitem__(
                (o, pl.ds(start, BLOCK), pl.ds(128 * j, 128)), value
            ),
            regroup_scratch,
            8,
        )
        return carry

    lax.fori_loop(0, BLOCKS, regroup_m2m, 0)

    total = jnp.zeros((64, ROWS), F32)
    for k in range(8):
        rows = [own[pl.ds(4 * k + j, 64, stride=32), :].astype(BF16) for j in range(4)]
        total += nt(jnp.concatenate(rows, axis=1), wm[k, 0:ROWS, :])
    total = total.astype(BF16).astype(F32)
    for j in range(4):
        wide = min(128, ROWS - 128 * j)
        mids[j][:, 0:wide] = total[:, 128 * j : 128 * j + wide]
    total = jnp.zeros((8, ROWS), F32)
    for k in range(8):
        rows = [mids[j][pl.ds(k, 8, stride=8), :].astype(BF16) for j in range(4)]
        total += nt(jnp.concatenate(rows, axis=1), wm[k, 0:ROWS, :])
    for j in range(4):
        wide = min(128, ROWS - 128 * j)
        top[pl.ds(j, 8, stride=4), 0:wide] = total[:, 128 * j : 128 * j + wide]
    topb[...] = top[...].astype(BF16)

    mine = pltpu.make_async_copy(topb, mt.at[yz, core, pl.ds(sx * 32, 32)], misc.at[2])
    mine.start()

    def gather_copy(number, step):
        if number == 0:
            src, dst = topb, mt.at[yz, core, pl.ds(sx * 32, 32)]
        elif number == 1:
            src = dst = mt.at[pl.ds(sy * 4, 4), core, pl.ds(sx * 32, 32)]
        elif number == 2:
            src = dst = mt.at[pl.ds(sy * 4, 4), core]
        else:
            src = dst = mt.at[:, core]
        index = number * 3 + step - 1
        return pltpu.make_async_remote_copy(
            src_ref=src,
            dst_ref=dst,
            send_sem=a_send.at[index],
            recv_sem=a_recv.at[index],
            device_id=group_peer(number, step),
            device_id_type=MESH,
        )

    for step in (1, 2, 3):
        gather_copy(0, step).start()
    give(6, 10)
    for number, first, last in ((1, 10, 14), (2, 14, 20), (3, 20, DIRS)):
        for step in (1, 2, 3):
            gather_copy(number - 1, step).wait()
        if number == 1:
            mine.wait()
        for step in (1, 2, 3) if number < 3 else (1,):
            gather_copy(number, step).start()
        give(first, last)
    places = lax.broadcasted_iota(jnp.int32, (8, TOPS), 1)
    wanted = jnp.where(cmask[...] == 1, csrc[...], -1)
    chosen = [(wanted[:, o : o + 1] == places).astype(F32) for o in range(OPS)]
    chosen = jnp.concatenate(chosen, axis=0).astype(BF16)
    gather_copy(3, 1).wait()

    wide_top[...] = mt[...].reshape(4 * TOPS, 128).astype(F32)
    tops = [wide_top[pl.ds(j, TOPS, stride=4), :].astype(BF16) for j in range(4)]
    sources = jnp.dot(chosen, jnp.concatenate(tops, axis=1), preferred_element_type=F32)
    w_copy.wait()
    l_top = jnp.zeros((8, COEF), F32)
    for c in range(CHUNKS):
        left = [sources[8 * (CHUNK * c + q) : 8 * (CHUNK * c + q) + 8] for q in range(CHUNK)]
        right = [widen(w[CHUNK * c + q]) for q in range(CHUNK)]
        l_top += nt(jnp.concatenate(left, axis=1).astype(BF16), jnp.concatenate(right, axis=1))
    l_top = (0.25 * l_top).astype(BF16)

    l2l_copy.wait()
    for k in range(8):
        part = nt(l_top, l2l_vm[k])
        for j in range(4):
            wide = chunk_width(j)
            mids[j][pl.ds(k, 8, stride=8), 0:wide] = part[:, 128 * j : 128 * j + wide]
    l_mid = [mids[j][:, 0 : chunk_width(j)] for j in range(4)]
    l_mid = jnp.concatenate(l_mid, axis=1).astype(BF16)
    far[3] = jnp.zeros((BOXES, 128), F32)
    for k in range(8):
        part = nt(l_mid, l2l_vm[k])
        for j in range(4):
            wide = chunk_width(j)
            far[j, pl.ds(k, 64, stride=8), 0:wide] = part[:, 128 * j : 128 * j + wide]

    far_copy = pltpu.make_async_copy(far, far_hbm, out_sem.at[2])
    far_copy.start()
    for j in range(DIRS):
        ghost_copy(j).wait()
    own_copy.wait()
    idx_copy.wait()
    far_copy.wait()


def block(array):
    return pl.BlockSpec(array.shape, lambda s: (0,) * array.ndim)


def prepare(multipoles, gh, slot, mask, csrc, cmask, m2m_ops, m2l_ops, l2l_ops):
    any_space = pl.BlockSpec(memory_space=pl.ANY)
    return pl.pallas_call(
        prep,
        out_shape=(
            jax.ShapeDtypeStruct((4 * BOXES, 128), F32),
            jax.ShapeDtypeStruct((OPS, 1, BOXES), jnp.int32),
            jax.ShapeDtypeStruct((4, BOXES, 128), F32),
            jax.ShapeDtypeStruct((GHOST * DIRS, WIDE), BF16),
        ),
        in_specs=[any_space] * 9,
        out_specs=(any_space,) * 4,
        scratch_shapes=[pltpu.VMEM(a.shape, a.dtype) for a in (multipoles, gh, slot, mask, csrc, cmask)]
        + [
            pltpu.VMEM((4 * BOXES, 128), F32),
            pltpu.VMEM((OPS, 1, BOXES), jnp.int32),
            pltpu.VMEM((4, BOXES, 128), F32),
            pltpu.VMEM((DIRS, GHOST, WIDE), BF16),
            pltpu.VMEM((BLOCK * BLOCKS, 8, COEF), BF16),
            pltpu.VMEM((8, BLOCK * BLOCKS, WIDE), BF16),
            pltpu.VMEM((8, COEF, COEF), BF16),
            pltpu.VMEM((OPS, COEF, COEF), BF16),
            pltpu.VMEM((32, 128), F32),
        ]
        + [pltpu.VMEM((8 * BLOCK, 128), F32)] * 4
        + [pltpu.VMEM((64, 128), F32)] * 4
        + [
            pltpu.VMEM((32, 128), F32),
            pltpu.VMEM((32, 128), BF16),
            pltpu.VMEM((16, 2, 128, 128), BF16),
            pltpu.VMEM((4 * TOPS, 128), F32),
            pltpu.SemaphoreType.DMA((DIRS,)),
            pltpu.SemaphoreType.DMA((DIRS,)),
            pltpu.SemaphoreType.DMA((10,)),
            pltpu.SemaphoreType.DMA((10,)),
            pltpu.SemaphoreType.DMA((6,)),
            pltpu.SemaphoreType.DMA((3,)),
            pltpu.SemaphoreType.DMA((4,)),
        ],
        compiler_params=pltpu.CompilerParams(
            collective_id=0, has_side_effects=True, vmem_limit_bytes=58 * 2**20
        ),
    )(multipoles, gh, slot, mask, csrc, cmask, m2m_ops, m2l_ops, l2l_ops)


def translate(idx, own, far, ghost, w, out, table, even, odd, acc):
    s = pl.program_id(0)

    def collect(pair, buf):
        for q in range(2):
            o = pair * 2 + q
            for first in range(0, BOXES, 8):
                rows = [
                    table[pl.ds(pl.multiple_of(idx[o, 0, first + u], 4), 4), :] for u in range(8)
                ]
                for u in range(8):
                    buf[q, pl.ds(4 * (first + u), 4), :] = rows[u]

    def multiply(buf, first):
        left = [
            buf[q, pl.ds(j, BOXES, stride=4), :].astype(BF16) for q in range(2) for j in range(4)
        ]
        right = [widen(w[first + q]) for q in range(2)]
        acc[...] += nt(jnp.concatenate(left, axis=1), jnp.concatenate(right, axis=1))

    @pl.when(s == 0)
    def _():
        for j in range(4):
            wide = chunk_width(j)
            acc[:, 128 * j : 128 * j + wide] = far[j, :, 0:wide]
            received = ghost[:, 128 * j : 128 * (j + 1)].astype(F32)
            table[pl.ds(4 * BOXES + j, GHOST * DIRS, stride=4), :] = received
        table[0 : 4 * BOXES, :] = own[...]
        table[4 * EMPTY : 4 * TABLE, :] = jnp.zeros((4 * (TABLE - EMPTY), 128), F32)
        collect(0, even)

    collect(2 * s + 1, odd)
    multiply(even, 0)

    @pl.when(s < CHUNKS - 1)
    def _():
        collect(2 * s + 2, even)
        multiply(odd, 2)

    @pl.when(s == CHUNKS - 1)
    def _():
        multiply(odd, 2)
        out[...] = acc[...].T.astype(BF16)


def apply_near(idx, own, far, ghost, w):
    return pl.pallas_call(
        translate,
        grid=(CHUNKS,),
        out_shape=jax.ShapeDtypeStruct((COEF, BOXES), BF16),
        in_specs=[
            pl.BlockSpec(memory_space=pltpu.SMEM),
            block(own),
            block(far),
            block(ghost),
            pl.BlockSpec((CHUNK, COEF, COEF), lambda s: (s, 0, 0)),
        ],
        out_specs=pl.BlockSpec((COEF, BOXES), lambda s: (0, 0)),
        scratch_shapes=[pltpu.VMEM((4 * TABLE, 128), F32)]
        + [pltpu.VMEM((2, 4 * BOXES, 128), F32)] * 2
        + [pltpu.VMEM((BOXES, COEF), F32)],
        compiler_params=pltpu.CompilerParams(vmem_limit_bytes=58 * 2**20),
    )(idx, own, far, ghost, w)


def local(
    multipoles,
    m2l_ops,
    m2m_ops,
    l2l_ops,
    ghost_rows,
    source_slot,
    pair_mask,
    coarse_src,
    coarse_mask,
):
    by_class = jnp.transpose(m2l_ops, (1, 0, 2))
    own, idx, far, ghost = prepare(
        multipoles,
        jnp.transpose(ghost_rows, (1, 0, 2)),
        jnp.transpose(source_slot, (1, 0, 2)),
        jnp.transpose(pair_mask, (1, 0, 2)),
        coarse_src,
        coarse_mask,
        m2m_ops,
        by_class,
        l2l_ops,
    )
    return apply_near(idx, own, far, ghost, by_class)


def solution(mesh):
    both = ("leaf", "sub")
    return jax.shard_map(
        local,
        mesh=mesh,
        in_specs=(
            P(None, both),
            P(),
            P(),
            P(),
            P(both, None, None),
            P(both, None, None),
            P(both, None, None),
            P(both, None),
            P(both, None),
        ),
        out_specs=P(None, both),
        check_vma=False,
    )
```

```python
import functools

import jax
import jax.numpy as jnp
from jax import lax
from jax.experimental import pallas as pl
from jax.experimental.pallas import tpu as pltpu
from jax.sharding import PartitionSpec as P

MESH = pl.DeviceIdType.MESH
COEF = 456
WIDE = 512
ROWS = 464
OPS = 44
BOXES = 512
GHOST = 64
DIRS = 26
RANKS = 128
SLOTS = 2176
EMPTY = SLOTS
TOP = SLOTS + 8
TOPS = 1024
TABLE = TOP + TOPS
TARGETS = BOXES + 8
PADDED = 528
BLOCK = 48
BLOCKS = 10
CHUNK = 4
CHUNKS = OPS // CHUNK
ORDER = [j for i in range(9) for j in (i, 17 + i, 9 + i)][:DIRS]
F32 = jnp.float32
BF16 = jnp.bfloat16


def place(d):
    return (d // 4, d % 4)


def chunk_width(j):
    return min(128, COEF - 128 * j)


def regroup(load, store, scratch, classes):
    for first in range(0, classes, 8):
        here = min(8, classes - first)
        for j in range(4):
            wide = chunk_width(j)
            part = load(first, here, j, wide).astype(F32)
            if here < 8:
                part = jnp.concatenate([part, jnp.zeros((BLOCK, 8 - here, wide), F32)], axis=1)
            scratch[j][:, 0:wide] = part.reshape(BLOCK * 8, wide)
        for o in range(here):
            for j in range(4):
                store(first + o, j, scratch[j][pl.ds(o, BLOCK, stride=8), :].astype(BF16))


def widen(w):
    tail = jnp.concatenate([w[:, 384:COEF], jnp.zeros((COEF, WIDE - COEF), BF16)], axis=1)
    return jnp.concatenate([w[:, 0:384], tail], axis=1)


def nt(left, right):
    return lax.dot_general(left, right, (((1,), (1,)), ((), ())), preferred_element_type=F32)


def prep(
    x_hbm,
    gh_hbm,
    slot_hbm,
    mask_hbm,
    csrc_hbm,
    cmask_hbm,
    m2m,
    own_hbm,
    idx_hbm,
    mt,
    ghost,
    x,
    gh,
    slot,
    mask,
    csrc,
    cmask,
    own,
    idx,
    send,
    m2m_vm,
    wm,
    picks,
    r0,
    r1,
    r2,
    r3,
    mid0,
    mid1,
    mid2,
    mid3,
    top,
    topb,
    g_send,
    g_recv,
    a_send,
    a_recv,
    in_sem,
    out_sem,
    misc,
):
    leaf = lax.axis_index("leaf")
    sx = lax.axis_index("sub")
    me = leaf * 4 + sx
    core = leaf % 2
    yz = leaf // 2
    sz = yz % 4
    sy = yz // 4
    regroup_scratch = (r0, r1, r2, r3)
    mids = (mid0, mid1, mid2, mid3)

    def offset(j):
        k = j + jnp.where(j >= 13, 1, 0)
        return 16 * (k // 9 - 1) + 4 * ((k // 3) % 3 - 1) + (k % 3 - 1)

    def reader(j):
        return place((me - offset(j) + RANKS) % RANKS)

    def row_peer(step):
        return ((sy * 4 + (sz + step) % 4) * 2 + core, sx)

    def plane_peer(step):
        return ((((sy + step // 4) % 4) * 4 + sz) * 2 + core, (sx + step % 4) % 4)

    twin = (yz * 2 + (1 - core), sx)

    barrier = pltpu.get_barrier_semaphore()

    def greet(i, carry):
        pl.semaphore_signal(barrier, inc=1, device_id=reader(i), device_id_type=MESH)
        return carry

    lax.fori_loop(0, DIRS, greet, 0)
    for step in (1, 2, 3):
        pl.semaphore_signal(barrier, inc=1, device_id=row_peer(step), device_id_type=MESH)

    def greet_plane(step, carry):
        pl.semaphore_signal(barrier, inc=1, device_id=plane_peer(step), device_id_type=MESH)
        return carry

    lax.fori_loop(1, 16, greet_plane, 0)
    pl.semaphore_signal(barrier, inc=1, device_id=twin, device_id_type=MESH)

    given = (x_hbm, gh_hbm, slot_hbm, mask_hbm, csrc_hbm, cmask_hbm)
    small = [
        pltpu.make_async_copy(source, target, in_sem.at[n])
        for n, (source, target) in enumerate(zip(given, (x, gh, slot, mask, csrc, cmask)))
    ]
    for copy in small:
        copy.start()
    m2m_copy = pltpu.make_async_copy(m2m, m2m_vm.at[pl.ds(0, COEF)], misc.at[0])
    m2m_copy.start()
    r3[...] = jnp.zeros_like(r3)
    mid3[...] = jnp.zeros_like(mid3)
    top[...] = jnp.zeros_like(top)
    m2m_vm[COEF : BLOCK * BLOCKS] = jnp.zeros((BLOCK * BLOCKS - COEF, 8, COEF), BF16)

    picks[...] = jnp.zeros_like(picks)
    for copy in small:
        copy.wait()
    for j in range(DIRS):
        picks[j : j + 1, 0:GHOST] = gh[j].astype(F32)
    by_direction = picks[...].T[0:GHOST]
    whole = jnp.concatenate([x[...].astype(F32), jnp.zeros((WIDE - COEF, BOXES), F32)], axis=0).T
    for j in range(4):
        own[pl.ds(j, BOXES, stride=4), :] = whole[:, 128 * j : 128 * (j + 1)]
    idx[:, :, 0:BOXES] = 4 * jnp.where(mask[...] == 1, slot[...], EMPTY)
    wanted = 4 * jnp.where(cmask[...] == 1, csrc[...] + TOP, EMPTY)
    picks[0:8, 0:OPS] = wanted.astype(F32)
    wanted = picks[...].T[0:OPS, 0:8].astype(jnp.int32)
    for o in range(OPS):
        idx[o, :, BOXES:TARGETS] = wanted[o : o + 1]
    own_copy = pltpu.make_async_copy(own, own_hbm, out_sem.at[0])
    idx_copy = pltpu.make_async_copy(idx, idx_hbm, out_sem.at[1])
    own_copy.start()
    idx_copy.start()

    pl.semaphore_wait(barrier, DIRS + 19)

    def ghost_copy(j):
        return pltpu.make_async_remote_copy(
            src_ref=send.at[j],
            dst_ref=ghost.at[pl.ds(j * GHOST, GHOST)],
            send_sem=g_send.at[j],
            recv_sem=g_recv.at[j],
            device_id=reader(j),
            device_id_type=MESH,
        )

    columns = whole.astype(BF16)
    lanes = lax.broadcasted_iota(jnp.int32, (GHOST, BOXES), 1).astype(F32)

    def give(first, last):
        group = ORDER[first:last]
        chosen = [(by_direction[:, j : j + 1] == lanes).astype(F32).astype(BF16) for j in group]
        rows = jnp.dot(jnp.concatenate(chosen, axis=0), columns, preferred_element_type=F32)
        for n, j in enumerate(group):
            send[j] = rows[GHOST * n : GHOST * (n + 1)].astype(BF16)
            ghost_copy(j).start()

    give(0, 6)
    m2m_copy.wait()

    def regroup_m2m(b, carry):
        start = pl.multiple_of(b * BLOCK, BLOCK)
        regroup(
            lambda first, here, j, wide: m2m_vm[
                pl.ds(start, BLOCK), pl.ds(first, here), pl.ds(128 * j, wide)
            ],
            lambda o, j, value: wm.__setitem__(
                (pl.ds(start, BLOCK), pl.ds(WIDE * o + 128 * j, 128)), value
            ),
            regroup_scratch,
            8,
        )
        return carry

    lax.fori_loop(0, BLOCKS, regroup_m2m, 0)

    rows = [own[pl.ds(4 * k + j, 64, stride=32), :] for k in range(8) for j in range(4)]
    total = nt(jnp.concatenate(rows, axis=1).astype(BF16), wm[0:ROWS, :])
    total = total.astype(BF16).astype(F32)
    for j in range(4):
        wide = min(128, ROWS - 128 * j)
        mids[j][:, 0:wide] = total[:, 128 * j : 128 * j + wide]
    rows = [mids[j][pl.ds(k, 8, stride=8), :] for k in range(8) for j in range(4)]
    total = nt(jnp.concatenate(rows, axis=1).astype(BF16), wm[0:ROWS, :])
    for j in range(4):
        wide = min(128, ROWS - 128 * j)
        top[pl.ds(j, 8, stride=4), 0:wide] = total[:, 128 * j : 128 * j + wide]
    topb[...] = top[...].astype(BF16)

    mine = pltpu.make_async_copy(topb, mt.at[yz, core, pl.ds(sx * 32, 32)], misc.at[2])
    mine.start()

    def share(src, dst, index, peer):
        return pltpu.make_async_remote_copy(
            src_ref=src,
            dst_ref=dst,
            send_sem=a_send.at[index],
            recv_sem=a_recv.at[index],
            device_id=peer,
            device_id_type=MESH,
        )

    def row_copy(step):
        return share(topb, mt.at[yz, core, pl.ds(sx * 32, 32)], step, row_peer(step))

    def plane_copy(step):
        part = mt.at[pl.ds(sy * 4, 4), core, pl.ds(sx * 32, 32)]
        return share(part, part, 3 + step, plane_peer(step))

    def twin_copy():
        return share(mt.at[:, core], mt.at[:, core], 0, twin)

    for step in (1, 2, 3):
        row_copy(step).start()
    give(6, 10)
    mine.wait()
    for step in (1, 2, 3):
        row_copy(step).wait()

    def plane_start(step, carry):
        plane_copy(step).start()
        return carry

    def plane_wait(step, carry):
        plane_copy(step).wait()
        return carry

    lax.fori_loop(1, 16, plane_start, 0)
    give(10, 18)
    lax.fori_loop(1, 16, plane_wait, 0)
    twin_copy().start()
    give(18, DIRS)
    twin_copy().wait()
    for j in range(DIRS):
        ghost_copy(j).wait()
    own_copy.wait()
    idx_copy.wait()


def block(array):
    return pl.BlockSpec(array.shape, lambda s: (0,) * array.ndim)


def prepare(multipoles, gh, slot, mask, csrc, cmask, m2m_ops):
    any_space = pl.BlockSpec(memory_space=pl.ANY)
    return pl.pallas_call(
        prep,
        out_shape=(
            jax.ShapeDtypeStruct((4 * BOXES, 128), F32),
            jax.ShapeDtypeStruct((OPS, 1, TARGETS), jnp.int32),
            jax.ShapeDtypeStruct((16, 2, 128, 128), BF16),
            jax.ShapeDtypeStruct((GHOST * DIRS, WIDE), BF16),
        ),
        in_specs=[any_space] * 7,
        out_specs=(any_space,) * 4,
        scratch_shapes=[pltpu.VMEM(a.shape, a.dtype) for a in (multipoles, gh, slot, mask, csrc, cmask)]
        + [
            pltpu.VMEM((4 * BOXES, 128), F32),
            pltpu.VMEM((OPS, 1, TARGETS), jnp.int32),
            pltpu.VMEM((DIRS, GHOST, WIDE), BF16),
            pltpu.VMEM((BLOCK * BLOCKS, 8, COEF), BF16),
            pltpu.VMEM((BLOCK * BLOCKS, 8 * WIDE), BF16),
            pltpu.VMEM((32, 128), F32),
        ]
        + [pltpu.VMEM((8 * BLOCK, 128), F32)] * 4
        + [pltpu.VMEM((64, 128), F32)] * 4
        + [
            pltpu.VMEM((32, 128), F32),
            pltpu.VMEM((32, 128), BF16),
            pltpu.SemaphoreType.DMA((DIRS,)),
            pltpu.SemaphoreType.DMA((DIRS,)),
            pltpu.SemaphoreType.DMA((19,)),
            pltpu.SemaphoreType.DMA((19,)),
            pltpu.SemaphoreType.DMA((6,)),
            pltpu.SemaphoreType.DMA((2,)),
            pltpu.SemaphoreType.DMA((3,)),
        ],
        compiler_params=pltpu.CompilerParams(
            collective_id=0, has_side_effects=True, vmem_limit_bytes=58 * 2**20
        ),
    )(multipoles, gh, slot, mask, csrc, cmask, m2m_ops)


def translate(idx, own, mt, ghost, w, l2l_hbm, out, table, even, odd, acc, l2l, l2l_sem, *far):
    s = pl.program_id(0)
    l2l_copy = pltpu.make_async_copy(l2l_hbm, l2l, l2l_sem)

    def collect(pair, buf):
        for q in range(2):
            o = pair * 2 + q
            for first in range(0, TARGETS, 8):
                rows = [
                    table[pl.ds(pl.multiple_of(idx[o, 0, first + u], 4), 4), :] for u in range(8)
                ]
                for u in range(8):
                    buf[q, pl.ds(4 * (first + u), 4), :] = rows[u]

    def multiply(buf, first):
        left = [
            buf[q, pl.ds(j, PADDED, stride=4), :].astype(BF16) for q in range(2) for j in range(4)
        ]
        right = [widen(w[first + q]) for q in range(2)]
        acc[...] += nt(jnp.concatenate(left, axis=1), jnp.concatenate(right, axis=1))

    @pl.when(s == 0)
    def _():
        l2l_copy.start()
        even[...] = jnp.zeros_like(even)
        odd[...] = jnp.zeros_like(odd)
        acc[...] = jnp.zeros_like(acc)
        for j in range(4):
            received = ghost[:, 128 * j : 128 * (j + 1)].astype(F32)
            table[pl.ds(4 * BOXES + j, GHOST * DIRS, stride=4), :] = received
        table[0 : 4 * BOXES, :] = own[...]
        table[4 * EMPTY : 4 * TOP, :] = jnp.zeros((4 * (TOP - EMPTY), 128), F32)
        table[4 * TOP : 4 * TABLE, :] = mt[...].reshape(4 * TOPS, 128).astype(F32)
        collect(0, even)

    collect(2 * s + 1, odd)
    multiply(even, 0)

    @pl.when(s < CHUNKS - 1)
    def _():
        collect(2 * s + 2, even)
        multiply(odd, 2)

    @pl.when(s == CHUNKS - 1)
    def _():
        multiply(odd, 2)
        l2l_copy.wait()
        l_top = (0.25 * acc[BOXES:PADDED, :]).astype(BF16)
        for k in range(8):
            part = nt(l_top, l2l[k])[0:8]
            for j in range(4):
                wide = chunk_width(j)
                far[j][pl.ds(k, 8, stride=8), 0:wide] = part[:, 128 * j : 128 * j + wide]
        l_mid = jnp.concatenate([far[j][0:64, 0 : chunk_width(j)] for j in range(4)], axis=1)
        l_mid = l_mid.astype(BF16)
        for k in range(8):
            part = nt(l_mid, l2l[k])
            for j in range(4):
                wide = chunk_width(j)
                far[j][pl.ds(k, 64, stride=8), 0:wide] = part[:, 128 * j : 128 * j + wide]
        for j in range(4):
            wide = chunk_width(j)
            both = acc[0:BOXES, 128 * j : 128 * j + wide] + far[j][:, 0:wide]
            out[128 * j : 128 * j + wide, :] = both.T.astype(BF16)


def apply_near(idx, own, mt, ghost, w, l2l_ops):
    return pl.pallas_call(
        translate,
        grid=(CHUNKS,),
        out_shape=jax.ShapeDtypeStruct((COEF, BOXES), BF16),
        in_specs=[
            pl.BlockSpec(memory_space=pltpu.SMEM),
            block(own),
            block(mt),
            block(ghost),
            pl.BlockSpec((CHUNK, COEF, COEF), lambda s: (s, 0, 0)),
            pl.BlockSpec(memory_space=pl.ANY),
        ],
        out_specs=pl.BlockSpec((COEF, BOXES), lambda s: (0, 0)),
        scratch_shapes=[pltpu.VMEM((4 * TABLE, 128), F32)]
        + [pltpu.VMEM((2, 4 * PADDED, 128), F32)] * 2
        + [
            pltpu.VMEM((PADDED, COEF), F32),
            pltpu.VMEM((8, COEF, COEF), BF16),
            pltpu.SemaphoreType.DMA,
        ]
        + [pltpu.VMEM((BOXES, 128), F32)] * 4,
        compiler_params=pltpu.CompilerParams(vmem_limit_bytes=58 * 2**20),
    )(idx, own, mt, ghost, w, l2l_ops)


def local(
    multipoles,
    m2l_ops,
    m2m_ops,
    l2l_ops,
    ghost_rows,
    source_slot,
    pair_mask,
    coarse_src,
    coarse_mask,
):
    by_class = jnp.transpose(m2l_ops, (1, 0, 2))
    own, idx, mt, ghost = prepare(
        multipoles,
        jnp.transpose(ghost_rows, (1, 0, 2)),
        jnp.transpose(source_slot, (1, 0, 2)),
        jnp.transpose(pair_mask, (1, 0, 2)),
        coarse_src,
        coarse_mask,
        m2m_ops,
    )
    return apply_near(idx, own, mt, ghost, by_class, l2l_ops)


def solution(mesh):
    both = ("leaf", "sub")
    return jax.shard_map(
        local,
        mesh=mesh,
        in_specs=(
            P(None, both),
            P(),
            P(),
            P(),
            P(both, None, None),
            P(both, None, None),
            P(both, None, None),
            P(both, None),
            P(both, None),
        ),
        out_specs=P(None, both),
        check_vma=False,
    )
```

```python
import functools

import jax
import jax.numpy as jnp
from jax import lax
from jax.experimental import pallas as pl
from jax.experimental.pallas import tpu as pltpu
from jax.sharding import PartitionSpec as P

MESH = pl.DeviceIdType.MESH
COEF = 456
WIDE = 512
ROWS = 464
OPS = 44
BOXES = 512
GHOST = 64
DIRS = 26
RANKS = 128
SLOTS = 2176
EMPTY = SLOTS
TOP = SLOTS + 8
TOPS = 1024
TABLE = TOP + TOPS
TARGETS = BOXES + 8
FIRST = 8
FLIGHT = 6
PADDED = 528
BLOCK = 48
BLOCKS = 10
CHUNK = 4
CHUNKS = OPS // CHUNK
ORDER = [j for i in range(9) for j in (i, 17 + i, 9 + i)][:DIRS]
F32 = jnp.float32
BF16 = jnp.bfloat16


def place(d):
    return (d // 4, d % 4)


def chunk_width(j):
    return min(128, COEF - 128 * j)


def regroup(load, store, scratch, classes):
    for first in range(0, classes, 8):
        here = min(8, classes - first)
        for j in range(4):
            wide = chunk_width(j)
            part = load(first, here, j, wide).astype(F32)
            if here < 8:
                part = jnp.concatenate([part, jnp.zeros((BLOCK, 8 - here, wide), F32)], axis=1)
            scratch[j][:, 0:wide] = part.reshape(BLOCK * 8, wide)
        for o in range(here):
            for j in range(4):
                store(first + o, j, scratch[j][pl.ds(o, BLOCK, stride=8), :].astype(BF16))


def widen(w):
    tail = jnp.concatenate([w[:, 384:COEF], jnp.zeros((COEF, WIDE - COEF), BF16)], axis=1)
    return jnp.concatenate([w[:, 0:384], tail], axis=1)


def nt(left, right):
    return lax.dot_general(left, right, (((1,), (1,)), ((), ())), preferred_element_type=F32)


def prep(
    x_hbm,
    gh_hbm,
    slot_hbm,
    mask_hbm,
    csrc_hbm,
    cmask_hbm,
    m2m,
    own_hbm,
    idx_hbm,
    mt,
    ghost,
    x,
    gh,
    slot,
    mask,
    csrc,
    cmask,
    own,
    idx,
    send,
    m2m_vm,
    wm,
    picks,
    r0,
    r1,
    r2,
    r3,
    mid0,
    mid1,
    mid2,
    mid3,
    top,
    topb,
    g_send,
    g_recv,
    a_send,
    a_recv,
    in_sem,
    out_sem,
    misc,
):
    leaf = lax.axis_index("leaf")
    sx = lax.axis_index("sub")
    me = leaf * 4 + sx
    core = leaf % 2
    yz = leaf // 2
    sz = yz % 4
    sy = yz // 4
    regroup_scratch = (r0, r1, r2, r3)
    mids = (mid0, mid1, mid2, mid3)

    def offset(j):
        k = j + jnp.where(j >= 13, 1, 0)
        return 16 * (k // 9 - 1) + 4 * ((k // 3) % 3 - 1) + (k % 3 - 1)

    def reader(j):
        return place((me - offset(j) + RANKS) % RANKS)

    def row_peer(step):
        return ((sy * 4 + (sz + step) % 4) * 2 + core, sx)

    def plane_peer(step):
        return ((((sy + step // 4) % 4) * 4 + sz) * 2 + core, (sx + step % 4) % 4)

    twin = (yz * 2 + (1 - core), sx)

    barrier = pltpu.get_barrier_semaphore()

    def greet(i, carry):
        pl.semaphore_signal(barrier, inc=1, device_id=reader(i), device_id_type=MESH)
        return carry

    lax.fori_loop(0, DIRS, greet, 0)
    for step in (1, 2, 3):
        pl.semaphore_signal(barrier, inc=1, device_id=row_peer(step), device_id_type=MESH)

    def greet_plane(step, carry):
        pl.semaphore_signal(barrier, inc=1, device_id=plane_peer(step), device_id_type=MESH)
        return carry

    lax.fori_loop(1, 16, greet_plane, 0)
    pl.semaphore_signal(barrier, inc=1, device_id=twin, device_id_type=MESH)

    given = (x_hbm, gh_hbm, slot_hbm, mask_hbm, csrc_hbm, cmask_hbm)
    small = [
        pltpu.make_async_copy(source, target, in_sem.at[n])
        for n, (source, target) in enumerate(zip(given, (x, gh, slot, mask, csrc, cmask)))
    ]
    for copy in small:
        copy.start()
    m2m_copy = pltpu.make_async_copy(m2m, m2m_vm.at[pl.ds(0, COEF)], misc.at[0])
    m2m_copy.start()
    r3[...] = jnp.zeros_like(r3)
    mid3[...] = jnp.zeros_like(mid3)
    top[...] = jnp.zeros_like(top)
    m2m_vm[COEF : BLOCK * BLOCKS] = jnp.zeros((BLOCK * BLOCKS - COEF, 8, COEF), BF16)

    picks[...] = jnp.zeros_like(picks)
    for copy in small:
        copy.wait()
    for j in range(DIRS):
        picks[j : j + 1, 0:GHOST] = gh[j].astype(F32)
    by_direction = picks[...].T[0:GHOST]
    whole = jnp.concatenate([x[...].astype(F32), jnp.zeros((WIDE - COEF, BOXES), F32)], axis=0).T
    for j in range(4):
        own[pl.ds(j, BOXES, stride=4), :] = whole[:, 128 * j : 128 * (j + 1)]
    shift = FIRST - 4 * (lax.broadcasted_iota(jnp.int32, (1, 1, BOXES), 2) % 2)
    idx[:, :, 0:BOXES] = 4 * jnp.where(mask[...] == 1, slot[...], EMPTY) + shift
    wanted = 4 * jnp.where(cmask[...] == 1, csrc[...] + TOP, EMPTY)
    picks[0:8, 0:OPS] = wanted.astype(F32)
    wanted = picks[...].T[0:OPS, 0:8].astype(jnp.int32)
    for o in range(OPS):
        idx[o, :, BOXES:TARGETS] = wanted[o : o + 1] + shift[0, :, 0:8]
    own_copy = pltpu.make_async_copy(own, own_hbm, out_sem.at[0])
    idx_copy = pltpu.make_async_copy(idx, idx_hbm, out_sem.at[1])
    own_copy.start()
    idx_copy.start()

    pl.semaphore_wait(barrier, DIRS + 19)

    def ghost_copy(j):
        return pltpu.make_async_remote_copy(
            src_ref=send.at[j],
            dst_ref=ghost.at[pl.ds(j * GHOST, GHOST)],
            send_sem=g_send.at[j],
            recv_sem=g_recv.at[j],
            device_id=reader(j),
            device_id_type=MESH,
        )

    columns = whole.astype(BF16)
    lanes = lax.broadcasted_iota(jnp.int32, (GHOST, BOXES), 1).astype(F32)

    def give(first, last):
        group = ORDER[first:last]
        chosen = [(by_direction[:, j : j + 1] == lanes).astype(F32).astype(BF16) for j in group]
        rows = jnp.dot(jnp.concatenate(chosen, axis=0), columns, preferred_element_type=F32)
        for n, j in enumerate(group):
            send[j] = rows[GHOST * n : GHOST * (n + 1)].astype(BF16)
            if first + n >= FLIGHT:
                ghost_copy(ORDER[first + n - FLIGHT]).wait_send()
            ghost_copy(j).start()

    give(0, 9)
    m2m_copy.wait()

    def regroup_m2m(b, carry):
        start = pl.multiple_of(b * BLOCK, BLOCK)
        regroup(
            lambda first, here, j, wide: m2m_vm[
                pl.ds(start, BLOCK), pl.ds(first, here), pl.ds(128 * j, wide)
            ],
            lambda o, j, value: wm.__setitem__(
                (pl.ds(start, BLOCK), pl.ds(WIDE * o + 128 * j, 128)), value
            ),
            regroup_scratch,
            8,
        )
        return carry

    lax.fori_loop(0, BLOCKS, regroup_m2m, 0)

    rows = [own[pl.ds(4 * k + j, 64, stride=32), :] for k in range(8) for j in range(4)]
    total = nt(jnp.concatenate(rows, axis=1).astype(BF16), wm[0:ROWS, :])
    total = total.astype(BF16).astype(F32)
    for j in range(4):
        wide = min(128, ROWS - 128 * j)
        mids[j][:, 0:wide] = total[:, 128 * j : 128 * j + wide]
    rows = [mids[j][pl.ds(k, 8, stride=8), :] for k in range(8) for j in range(4)]
    total = nt(jnp.concatenate(rows, axis=1).astype(BF16), wm[0:ROWS, :])
    for j in range(4):
        wide = min(128, ROWS - 128 * j)
        top[pl.ds(j, 8, stride=4), 0:wide] = total[:, 128 * j : 128 * j + wide]
    topb[...] = top[...].astype(BF16)

    mine = pltpu.make_async_copy(topb, mt.at[yz, core, pl.ds(sx * 32, 32)], misc.at[2])
    mine.start()

    def share(src, dst, index, peer):
        return pltpu.make_async_remote_copy(
            src_ref=src,
            dst_ref=dst,
            send_sem=a_send.at[index],
            recv_sem=a_recv.at[index],
            device_id=peer,
            device_id_type=MESH,
        )

    def row_copy(step):
        return share(topb, mt.at[yz, core, pl.ds(sx * 32, 32)], step, row_peer(step))

    def plane_copy(step):
        part = mt.at[pl.ds(sy * 4, 4), core, pl.ds(sx * 32, 32)]
        return share(part, part, 3 + step, plane_peer(step))

    def twin_copy():
        return share(mt.at[:, core], mt.at[:, core], 0, twin)

    for step in (1, 2, 3):
        row_copy(step).start()
    give(9, 15)
    mine.wait()
    for step in (1, 2, 3):
        row_copy(step).wait()

    def plane_start(step, carry):
        plane_copy(step).start()
        return carry

    def plane_wait(step, carry):
        plane_copy(step).wait()
        return carry

    lax.fori_loop(1, 16, plane_start, 0)
    give(15, DIRS)
    lax.fori_loop(1, 16, plane_wait, 0)
    twin_copy().start()
    twin_copy().wait()
    for j in ORDER[DIRS - FLIGHT :]:
        ghost_copy(j).wait_send()
    for j in range(DIRS):
        ghost_copy(j).wait_recv()
    own_copy.wait()
    idx_copy.wait()


def block(array):
    return pl.BlockSpec(array.shape, lambda s: (0,) * array.ndim)


def prepare(multipoles, gh, slot, mask, csrc, cmask, m2m_ops):
    any_space = pl.BlockSpec(memory_space=pl.ANY)
    return pl.pallas_call(
        prep,
        out_shape=(
            jax.ShapeDtypeStruct((4 * BOXES, 128), F32),
            jax.ShapeDtypeStruct((OPS, 1, TARGETS), jnp.int32),
            jax.ShapeDtypeStruct((16, 2, 128, 128), BF16),
            jax.ShapeDtypeStruct((GHOST * DIRS, WIDE), BF16),
        ),
        in_specs=[any_space] * 7,
        out_specs=(any_space,) * 4,
        scratch_shapes=[pltpu.VMEM(a.shape, a.dtype) for a in (multipoles, gh, slot, mask, csrc, cmask)]
        + [
            pltpu.VMEM((4 * BOXES, 128), F32),
            pltpu.VMEM((OPS, 1, TARGETS), jnp.int32),
            pltpu.VMEM((DIRS, GHOST, WIDE), BF16),
            pltpu.VMEM((BLOCK * BLOCKS, 8, COEF), BF16),
            pltpu.VMEM((BLOCK * BLOCKS, 8 * WIDE), BF16),
            pltpu.VMEM((32, 128), F32),
        ]
        + [pltpu.VMEM((8 * BLOCK, 128), F32)] * 4
        + [pltpu.VMEM((64, 128), F32)] * 4
        + [
            pltpu.VMEM((32, 128), F32),
            pltpu.VMEM((32, 128), BF16),
            pltpu.SemaphoreType.DMA((DIRS,)),
            pltpu.SemaphoreType.DMA((DIRS,)),
            pltpu.SemaphoreType.DMA((19,)),
            pltpu.SemaphoreType.DMA((19,)),
            pltpu.SemaphoreType.DMA((6,)),
            pltpu.SemaphoreType.DMA((2,)),
            pltpu.SemaphoreType.DMA((3,)),
        ],
        compiler_params=pltpu.CompilerParams(
            collective_id=0, has_side_effects=True, vmem_limit_bytes=58 * 2**20
        ),
    )(multipoles, gh, slot, mask, csrc, cmask, m2m_ops)


def translate(idx, own, mt, ghost, w, l2l_hbm, out, table, even, odd, acc, l2l, l2l_sem, *far):
    s = pl.program_id(0)
    l2l_copy = pltpu.make_async_copy(l2l_hbm, l2l, l2l_sem)

    upper = lax.broadcasted_iota(jnp.int32, (8, 128), 0) < 4

    def collect(pair, buf):
        for q in range(2):
            o = pair * 2 + q
            for first in range(0, TARGETS, 8):
                rows = [
                    table[pl.ds(pl.multiple_of(idx[o, 0, first + u], 4), 8), :] for u in range(8)
                ]
                for u in range(0, 8, 2):
                    both = jnp.where(upper, rows[u], rows[u + 1])
                    buf[q, pl.ds(4 * (first + u), 8), :] = both

    def multiply(buf, first):
        left = [
            buf[q, pl.ds(j, PADDED, stride=4), :].astype(BF16) for q in range(2) for j in range(4)
        ]
        right = [widen(w[first + q]) for q in range(2)]
        acc[...] += nt(jnp.concatenate(left, axis=1), jnp.concatenate(right, axis=1))

    @pl.when(s == 0)
    def _():
        l2l_copy.start()
        for buf in (even, odd):
            buf[:, 4 * TARGETS :, :] = jnp.zeros((2, 4 * (PADDED - TARGETS), 128), F32)
        acc[...] = jnp.zeros_like(acc)
        for j in range(4):
            received = ghost[:, 128 * j : 128 * (j + 1)].astype(F32)
            table[pl.ds(FIRST + 4 * BOXES + j, GHOST * DIRS, stride=4), :] = received
        table[FIRST : FIRST + 4 * BOXES, :] = own[...]
        table[FIRST + 4 * EMPTY : FIRST + 4 * TOP, :] = jnp.zeros((4 * (TOP - EMPTY), 128), F32)
        table[FIRST + 4 * TOP : FIRST + 4 * TABLE, :] = mt[...].reshape(4 * TOPS, 128).astype(F32)
        collect(0, even)

    collect(2 * s + 1, odd)
    multiply(even, 0)

    @pl.when(s < CHUNKS - 1)
    def _():
        collect(2 * s + 2, even)
        multiply(odd, 2)

    @pl.when(s == CHUNKS - 1)
    def _():
        multiply(odd, 2)
        l2l_copy.wait()
        l_top = (0.25 * acc[BOXES:PADDED, :]).astype(BF16)
        for k in range(8):
            part = nt(l_top, l2l[k])[0:8]
            for j in range(4):
                wide = chunk_width(j)
                far[j][pl.ds(k, 8, stride=8), 0:wide] = part[:, 128 * j : 128 * j + wide]
        l_mid = jnp.concatenate([far[j][0:64, 0 : chunk_width(j)] for j in range(4)], axis=1)
        l_mid = l_mid.astype(BF16)
        for k in range(8):
            part = nt(l_mid, l2l[k])
            for j in range(4):
                wide = chunk_width(j)
                far[j][pl.ds(k, 64, stride=8), 0:wide] = part[:, 128 * j : 128 * j + wide]
        for j in range(4):
            wide = chunk_width(j)
            both = acc[0:BOXES, 128 * j : 128 * j + wide] + far[j][:, 0:wide]
            out[128 * j : 128 * j + wide, :] = both.T.astype(BF16)


def apply_near(idx, own, mt, ghost, w, l2l_ops):
    return pl.pallas_call(
        translate,
        grid=(CHUNKS,),
        out_shape=jax.ShapeDtypeStruct((COEF, BOXES), BF16),
        in_specs=[
            pl.BlockSpec(memory_space=pltpu.SMEM),
            block(own),
            block(mt),
            block(ghost),
            pl.BlockSpec((CHUNK, COEF, COEF), lambda s: (s, 0, 0)),
            pl.BlockSpec(memory_space=pl.ANY),
        ],
        out_specs=pl.BlockSpec((COEF, BOXES), lambda s: (0, 0)),
        scratch_shapes=[pltpu.VMEM((FIRST + 4 * TABLE + 8, 128), F32)]
        + [pltpu.VMEM((2, 4 * PADDED, 128), F32)] * 2
        + [
            pltpu.VMEM((PADDED, COEF), F32),
            pltpu.VMEM((8, COEF, COEF), BF16),
            pltpu.SemaphoreType.DMA,
        ]
        + [pltpu.VMEM((BOXES, 128), F32)] * 4,
        compiler_params=pltpu.CompilerParams(vmem_limit_bytes=58 * 2**20),
    )(idx, own, mt, ghost, w, l2l_ops)


def local(
    multipoles,
    m2l_ops,
    m2m_ops,
    l2l_ops,
    ghost_rows,
    source_slot,
    pair_mask,
    coarse_src,
    coarse_mask,
):
    by_class = jnp.transpose(m2l_ops, (1, 0, 2))
    own, idx, mt, ghost = prepare(
        multipoles,
        jnp.transpose(ghost_rows, (1, 0, 2)),
        jnp.transpose(source_slot, (1, 0, 2)),
        jnp.transpose(pair_mask, (1, 0, 2)),
        coarse_src,
        coarse_mask,
        m2m_ops,
    )
    return apply_near(idx, own, mt, ghost, by_class, l2l_ops)


def solution(mesh):
    both = ("leaf", "sub")
    return jax.shard_map(
        local,
        mesh=mesh,
        in_specs=(
            P(None, both),
            P(),
            P(),
            P(),
            P(both, None, None),
            P(both, None, None),
            P(both, None, None),
            P(both, None),
            P(both, None),
        ),
        out_specs=P(None, both),
        check_vma=False,
    )
```

```python
import functools

import jax
import jax.numpy as jnp
from jax import lax
from jax.experimental import pallas as pl
from jax.experimental.pallas import tpu as pltpu
from jax.sharding import PartitionSpec as P

MESH = pl.DeviceIdType.MESH
COEF = 456
WIDE = 512
ROWS = 464
OPS = 44
BOXES = 512
GHOST = 64
DIRS = 26
RANKS = 128
SLOTS = 2176
EMPTY = SLOTS
TOP = SLOTS + 8
TOPS = 1024
TABLE = TOP + TOPS
TARGETS = BOXES + 8
FIRST = 8
FLIGHT = 6
PADDED = 528
BLOCK = 48
BLOCKS = 10
CHUNK = 4
CHUNKS = OPS // CHUNK
STEPS = (-1, 0, 1)
OFFSETS = [o for o in (16 * a + 4 * b + c for a in STEPS for b in STEPS for c in STEPS) if o]
ORDER = [j for i in range(9) for j in (i, 17 + i, 9 + i)][:DIRS]
F32 = jnp.float32
BF16 = jnp.bfloat16


def place(d):
    return (lax.div(d, 4), lax.rem(d, 4))


def chunk_width(j):
    return min(128, COEF - 128 * j)


def regroup(load, store, scratch, classes):
    for first in range(0, classes, 8):
        here = min(8, classes - first)
        for j in range(4):
            wide = chunk_width(j)
            part = load(first, here, j, wide).astype(F32)
            if here < 8:
                part = jnp.concatenate([part, jnp.zeros((BLOCK, 8 - here, wide), F32)], axis=1)
            scratch[j][:, 0:wide] = part.reshape(BLOCK * 8, wide)
        for o in range(here):
            for j in range(4):
                store(first + o, j, scratch[j][pl.ds(o, BLOCK, stride=8), :].astype(BF16))


def widen(w):
    tail = jnp.concatenate([w[:, 384:COEF], jnp.zeros((COEF, WIDE - COEF), BF16)], axis=1)
    return jnp.concatenate([w[:, 0:384], tail], axis=1)


def nt(left, right):
    return lax.dot_general(left, right, (((1,), (1,)), ((), ())), preferred_element_type=F32)


def prep(
    x_hbm,
    gh_hbm,
    slot_hbm,
    mask_hbm,
    csrc_hbm,
    cmask_hbm,
    m2m,
    own_hbm,
    idx_hbm,
    mt,
    ghost,
    x,
    gh,
    slot,
    mask,
    csrc,
    cmask,
    own,
    idx,
    send,
    m2m_vm,
    wm,
    picks,
    r0,
    r1,
    r2,
    r3,
    mid0,
    mid1,
    mid2,
    mid3,
    top,
    topb,
    g_send,
    g_recv,
    a_send,
    a_recv,
    in_sem,
    out_sem,
    misc,
):
    leaf = lax.axis_index("leaf")
    sx = lax.axis_index("sub")
    me = leaf * 4 + sx
    core = lax.rem(leaf, 2)
    yz = lax.div(leaf, 2)
    sz = lax.rem(yz, 4)
    sy = lax.div(yz, 4)
    regroup_scratch = (r0, r1, r2, r3)
    mids = (mid0, mid1, mid2, mid3)

    def reader(j):
        return place(lax.rem(me + (RANKS - OFFSETS[j]), RANKS))

    def row_peer(step):
        return ((sy * 4 + lax.rem(sz + step, 4)) * 2 + core, sx)

    def plane_peer(step):
        y = lax.rem(sy + step // 4, 4)
        return ((y * 4 + sz) * 2 + core, lax.rem(sx + step % 4, 4))

    twin = (yz * 2 + (1 - core), sx)

    barrier = pltpu.get_barrier_semaphore()

    for j in range(DIRS):
        pl.semaphore_signal(barrier, inc=1, device_id=reader(j), device_id_type=MESH)
    for step in (1, 2, 3):
        pl.semaphore_signal(barrier, inc=1, device_id=row_peer(step), device_id_type=MESH)

    for step in range(1, 16):
        pl.semaphore_signal(barrier, inc=1, device_id=plane_peer(step), device_id_type=MESH)
    pl.semaphore_signal(barrier, inc=1, device_id=twin, device_id_type=MESH)

    given = (x_hbm, gh_hbm, slot_hbm, mask_hbm, csrc_hbm, cmask_hbm)
    small = [
        pltpu.make_async_copy(source, target, in_sem.at[n])
        for n, (source, target) in enumerate(zip(given, (x, gh, slot, mask, csrc, cmask)))
    ]
    for copy in small:
        copy.start()
    m2m_copy = pltpu.make_async_copy(m2m, m2m_vm.at[pl.ds(0, COEF)], misc.at[0])
    m2m_copy.start()
    r3[...] = jnp.zeros_like(r3)
    mid3[...] = jnp.zeros_like(mid3)
    top[...] = jnp.zeros_like(top)
    m2m_vm[COEF : BLOCK * BLOCKS] = jnp.zeros((BLOCK * BLOCKS - COEF, 8, COEF), BF16)

    picks[...] = jnp.zeros_like(picks)
    for copy in small:
        copy.wait()
    for j in range(DIRS):
        picks[j : j + 1, 0:GHOST] = gh[j].astype(F32)
    by_direction = picks[...].T[0:GHOST]
    whole = jnp.concatenate([x[...].astype(F32), jnp.zeros((WIDE - COEF, BOXES), F32)], axis=0).T
    for j in range(4):
        own[pl.ds(j, BOXES, stride=4), :] = whole[:, 128 * j : 128 * (j + 1)]
    own_copy = pltpu.make_async_copy(own, own_hbm, out_sem.at[0])
    own_copy.start()

    pl.semaphore_wait(barrier, DIRS + 19)

    def ghost_copy(j):
        return pltpu.make_async_remote_copy(
            src_ref=send.at[j],
            dst_ref=ghost.at[pl.ds(j * GHOST, GHOST)],
            send_sem=g_send.at[j],
            recv_sem=g_recv.at[j],
            device_id=reader(j),
            device_id_type=MESH,
        )

    columns = whole.astype(BF16)
    lanes = lax.broadcasted_iota(jnp.int32, (GHOST, BOXES), 1).astype(F32)

    def give(first, last):
        group = ORDER[first:last]
        chosen = [(by_direction[:, j : j + 1] == lanes).astype(F32).astype(BF16) for j in group]
        rows = jnp.dot(jnp.concatenate(chosen, axis=0), columns, preferred_element_type=F32)
        for n, j in enumerate(group):
            send[j] = rows[GHOST * n : GHOST * (n + 1)].astype(BF16)
            if first + n >= FLIGHT:
                ghost_copy(ORDER[first + n - FLIGHT]).wait_send()
            ghost_copy(j).start()

    give(0, 9)
    m2m_copy.wait()

    def regroup_m2m(b, carry):
        start = pl.multiple_of(b * BLOCK, BLOCK)
        regroup(
            lambda first, here, j, wide: m2m_vm[
                pl.ds(start, BLOCK), pl.ds(first, here), pl.ds(128 * j, wide)
            ],
            lambda o, j, value: wm.__setitem__(
                (pl.ds(start, BLOCK), pl.ds(WIDE * o + 128 * j, 128)), value
            ),
            regroup_scratch,
            8,
        )
        return carry

    lax.fori_loop(0, BLOCKS, regroup_m2m, 0)

    rows = [own[pl.ds(4 * k + j, 64, stride=32), :] for k in range(8) for j in range(4)]
    total = nt(jnp.concatenate(rows, axis=1).astype(BF16), wm[0:ROWS, :])
    total = total.astype(BF16).astype(F32)
    for j in range(4):
        wide = min(128, ROWS - 128 * j)
        mids[j][:, 0:wide] = total[:, 128 * j : 128 * j + wide]
    rows = [mids[j][pl.ds(k, 8, stride=8), :] for k in range(8) for j in range(4)]
    total = nt(jnp.concatenate(rows, axis=1).astype(BF16), wm[0:ROWS, :])
    for j in range(4):
        wide = min(128, ROWS - 128 * j)
        top[pl.ds(j, 8, stride=4), 0:wide] = total[:, 128 * j : 128 * j + wide]
    topb[...] = top[...].astype(BF16)

    mine = pltpu.make_async_copy(topb, mt.at[yz, core, pl.ds(sx * 32, 32)], misc.at[2])
    mine.start()

    def share(src, dst, index, peer):
        return pltpu.make_async_remote_copy(
            src_ref=src,
            dst_ref=dst,
            send_sem=a_send.at[index],
            recv_sem=a_recv.at[index],
            device_id=peer,
            device_id_type=MESH,
        )

    def row_copy(step):
        return share(topb, mt.at[yz, core, pl.ds(sx * 32, 32)], step, row_peer(step))

    def plane_copy(step):
        part = mt.at[pl.ds(sy * 4, 4), core, pl.ds(sx * 32, 32)]
        return share(part, part, 3 + step, plane_peer(step))

    def twin_copy():
        return share(mt.at[:, core], mt.at[:, core], 0, twin)

    for step in (1, 2, 3):
        row_copy(step).start()
    give(9, 15)
    mine.wait()
    for step in (1, 2, 3):
        row_copy(step).wait()

    for step in range(1, 16):
        plane_copy(step).start()
    give(15, DIRS)
    for step in range(1, 16):
        plane_copy(step).wait()
    twin_copy().start()
    shift = FIRST - 4 * (lax.broadcasted_iota(jnp.int32, (1, 1, BOXES), 2) % 2)
    idx[:, :, 0:BOXES] = 4 * jnp.where(mask[...] == 1, slot[...], EMPTY) + shift
    wanted = 4 * jnp.where(cmask[...] == 1, csrc[...] + TOP, EMPTY)
    picks[0:8, 0:OPS] = wanted.astype(F32)
    wanted = picks[...].T[0:OPS, 0:8].astype(jnp.int32)
    for o in range(OPS):
        idx[o, :, BOXES:TARGETS] = wanted[o : o + 1] + shift[0, :, 0:8]
    idx_copy = pltpu.make_async_copy(idx, idx_hbm, out_sem.at[1])
    idx_copy.start()
    twin_copy().wait()
    for j in ORDER[DIRS - FLIGHT :]:
        ghost_copy(j).wait_send()
    for j in range(DIRS):
        ghost_copy(j).wait_recv()
    own_copy.wait()
    idx_copy.wait()


def block(array):
    return pl.BlockSpec(array.shape, lambda s: (0,) * array.ndim)


def prepare(multipoles, gh, slot, mask, csrc, cmask, m2m_ops):
    any_space = pl.BlockSpec(memory_space=pl.ANY)
    return pl.pallas_call(
        prep,
        out_shape=(
            jax.ShapeDtypeStruct((4 * BOXES, 128), F32),
            jax.ShapeDtypeStruct((OPS, 1, TARGETS), jnp.int32),
            jax.ShapeDtypeStruct((16, 2, 128, 128), BF16),
            jax.ShapeDtypeStruct((GHOST * DIRS, WIDE), BF16),
        ),
        in_specs=[any_space] * 7,
        out_specs=(any_space,) * 4,
        scratch_shapes=[pltpu.VMEM(a.shape, a.dtype) for a in (multipoles, gh, slot, mask, csrc, cmask)]
        + [
            pltpu.VMEM((4 * BOXES, 128), F32),
            pltpu.VMEM((OPS, 1, TARGETS), jnp.int32),
            pltpu.VMEM((DIRS, GHOST, WIDE), BF16),
            pltpu.VMEM((BLOCK * BLOCKS, 8, COEF), BF16),
            pltpu.VMEM((BLOCK * BLOCKS, 8 * WIDE), BF16),
            pltpu.VMEM((32, 128), F32),
        ]
        + [pltpu.VMEM((8 * BLOCK, 128), F32)] * 4
        + [pltpu.VMEM((64, 128), F32)] * 4
        + [
            pltpu.VMEM((32, 128), F32),
            pltpu.VMEM((32, 128), BF16),
            pltpu.SemaphoreType.DMA((DIRS,)),
            pltpu.SemaphoreType.DMA((DIRS,)),
            pltpu.SemaphoreType.DMA((19,)),
            pltpu.SemaphoreType.DMA((19,)),
            pltpu.SemaphoreType.DMA((6,)),
            pltpu.SemaphoreType.DMA((2,)),
            pltpu.SemaphoreType.DMA((3,)),
        ],
        compiler_params=pltpu.CompilerParams(
            collective_id=0, has_side_effects=True, vmem_limit_bytes=58 * 2**20
        ),
    )(multipoles, gh, slot, mask, csrc, cmask, m2m_ops)


def translate(idx, own, mt, ghost, w, l2l_hbm, out, table, even, odd, acc, l2l, l2l_sem, *far):
    s = pl.program_id(0)
    l2l_copy = pltpu.make_async_copy(l2l_hbm, l2l, l2l_sem)

    upper = lax.broadcasted_iota(jnp.int32, (8, 128), 0) < 4

    def collect(pair, buf):
        for q in range(2):
            o = pair * 2 + q
            for first in range(0, TARGETS, 8):
                rows = [
                    table[pl.ds(pl.multiple_of(idx[o, 0, first + u], 4), 8), :] for u in range(8)
                ]
                for u in range(0, 8, 2):
                    both = jnp.where(upper, rows[u], rows[u + 1])
                    buf[q, pl.ds(4 * (first + u), 8), :] = both

    def multiply(buf, first):
        left = [
            buf[q, pl.ds(j, PADDED, stride=4), :].astype(BF16) for q in range(2) for j in range(4)
        ]
        right = [widen(w[first + q]) for q in range(2)]
        acc[...] += nt(jnp.concatenate(left, axis=1), jnp.concatenate(right, axis=1))

    @pl.when(s == 0)
    def _():
        l2l_copy.start()
        for buf in (even, odd):
            buf[:, 4 * TARGETS :, :] = jnp.zeros((2, 4 * (PADDED - TARGETS), 128), F32)
        acc[...] = jnp.zeros_like(acc)
        for j in range(4):
            received = ghost[:, 128 * j : 128 * (j + 1)].astype(F32)
            table[pl.ds(FIRST + 4 * BOXES + j, GHOST * DIRS, stride=4), :] = received
        table[FIRST : FIRST + 4 * BOXES, :] = own[...]
        table[FIRST + 4 * EMPTY : FIRST + 4 * TOP, :] = jnp.zeros((4 * (TOP - EMPTY), 128), F32)
        table[FIRST + 4 * TOP : FIRST + 4 * TABLE, :] = mt[...].reshape(4 * TOPS, 128).astype(F32)
        collect(0, even)

    collect(2 * s + 1, odd)
    multiply(even, 0)

    @pl.when(s < CHUNKS - 1)
    def _():
        collect(2 * s + 2, even)
        multiply(odd, 2)

    @pl.when(s == CHUNKS - 1)
    def _():
        multiply(odd, 2)
        l2l_copy.wait()
        l_top = (0.25 * acc[BOXES:PADDED, :]).astype(BF16)
        for k in range(8):
            part = nt(l_top, l2l[k])[0:8]
            for j in range(4):
                wide = chunk_width(j)
                far[j][pl.ds(k, 8, stride=8), 0:wide] = part[:, 128 * j : 128 * j + wide]
        l_mid = jnp.concatenate([far[j][0:64, 0 : chunk_width(j)] for j in range(4)], axis=1)
        l_mid = l_mid.astype(BF16)
        for k in range(8):
            part = nt(l_mid, l2l[k])
            for j in range(4):
                wide = chunk_width(j)
                far[j][pl.ds(k, 64, stride=8), 0:wide] = part[:, 128 * j : 128 * j + wide]
        for j in range(4):
            wide = chunk_width(j)
            both = acc[0:BOXES, 128 * j : 128 * j + wide] + far[j][:, 0:wide]
            out[128 * j : 128 * j + wide, :] = both.T.astype(BF16)


def apply_near(idx, own, mt, ghost, w, l2l_ops):
    return pl.pallas_call(
        translate,
        grid=(CHUNKS,),
        out_shape=jax.ShapeDtypeStruct((COEF, BOXES), BF16),
        in_specs=[
            pl.BlockSpec(memory_space=pltpu.SMEM),
            block(own),
            block(mt),
            block(ghost),
            pl.BlockSpec((CHUNK, COEF, COEF), lambda s: (s, 0, 0)),
            pl.BlockSpec(memory_space=pl.ANY),
        ],
        out_specs=pl.BlockSpec((COEF, BOXES), lambda s: (0, 0)),
        scratch_shapes=[pltpu.VMEM((FIRST + 4 * TABLE + 8, 128), F32)]
        + [pltpu.VMEM((2, 4 * PADDED, 128), F32)] * 2
        + [
            pltpu.VMEM((PADDED, COEF), F32),
            pltpu.VMEM((8, COEF, COEF), BF16),
            pltpu.SemaphoreType.DMA,
        ]
        + [pltpu.VMEM((BOXES, 128), F32)] * 4,
        compiler_params=pltpu.CompilerParams(vmem_limit_bytes=58 * 2**20),
    )(idx, own, mt, ghost, w, l2l_ops)


def local(
    multipoles,
    m2l_ops,
    m2m_ops,
    l2l_ops,
    ghost_rows,
    source_slot,
    pair_mask,
    coarse_src,
    coarse_mask,
):
    by_class = jnp.transpose(m2l_ops, (1, 0, 2))
    own, idx, mt, ghost = prepare(
        multipoles,
        jnp.transpose(ghost_rows, (1, 0, 2)),
        jnp.transpose(source_slot, (1, 0, 2)),
        jnp.transpose(pair_mask, (1, 0, 2)),
        coarse_src,
        coarse_mask,
        m2m_ops,
    )
    return apply_near(idx, own, mt, ghost, by_class, l2l_ops)


def solution(mesh):
    both = ("leaf", "sub")
    return jax.shard_map(
        local,
        mesh=mesh,
        in_specs=(
            P(None, both),
            P(),
            P(),
            P(),
            P(both, None, None),
            P(both, None, None),
            P(both, None, None),
            P(both, None),
            P(both, None),
        ),
        out_specs=P(None, both),
        check_vma=False,
    )
```
